32 devices in a mesh: tm: 2 (over x), height: 4 (over y, core), mp: 4 (over z).
Axes of the slice: x: 2, y: 2, z: 4, core: 2. Of those that a mesh axis runs over, the one named last changes fastest.
Arguments:
- image_q: bfloat16 [2, 4, 384, 3072], P('tm', 'height', None, 'mp'), may hold values from -8 to 8
- image_kv: bfloat16 [2, 4, 2, 384, 3072], P('tm', 'height', None, None, 'mp'), may hold values from -8 to 8
- text_kv: bfloat16 [2, 256, 3072], P(None, 'tm', 'mp'), may hold values from -8 to 8
- residual: bfloat16 [2, 4, 384, 3072], P('tm', 'height', None, 'mp'), may hold values from -3 to 3
- out_weight: bfloat16 [3072, 3072], P('mp'), may hold values from -0.109375 to 0.109375
- out_gate: float32 [3072], P('mp'), may hold values from 0.5 to 2
- head_reach: int32 [24, 2], P('mp'), may hold values from 0 to 1, as said below
- tile_extent: int32 [2, 2, 4], replicated, may hold values from 1 to 8, as said below
Outputs:
- updated_tokens: bfloat16 [2, 4, 384, 3072], P('tm', 'height', None, 'mp')
The draws below stay inside these ranges and needn't reach their ends.
Inputs may be any that keep to these rules, and one draw needn't show every extreme that they name: `head_reach`: in each column exactly 16 heads have reach 1, the others 0. `tile_extent`: valid frames are 6 except in the last tile row along time, where they are below 6; valid rows are 8 except in the last tile row along height, where they are below 8.
All inputs are finite; a program needn't handle non-finite values.
Results may differ from the reference program's by a relative error of at most 0.015.
Values may be sent and summed in bfloat16 or wider, within the bound.
A program may use at most 128 MiB of HBM per device.

```python
import math
import jax
import jax.numpy as jnp
from jax import lax

D = 3072
HEADS = 24
HD = 128
TXT = 256
TILE_F = 6
TILE_R = 8
TILE_C = 8
TILE = 384
TILES_T = 2
TILES_H = 4
HEAD_GROUPS = 4


def draw_image_q(key, part):
    full_shape = (TILES_T, TILES_H, TILE_F * TILE_R * TILE_C, HEADS * HD)
    base_key = jax.random.fold_in(key, 1)
    values = jnp.clip(1.6 * jax.random.normal(base_key, full_shape, jnp.float32), -8.0, 8.0)
    return values.astype(jnp.bfloat16)


def draw_image_kv(key, part):
    full_shape = (TILES_T, TILES_H, TILE_F * TILE_R * TILE_C, HEADS * HD)
    key_base = jax.random.fold_in(key, 2)
    value_base = jax.random.fold_in(key, 3)
    key_values = jnp.clip(1.6 * jax.random.normal(key_base, full_shape, jnp.float32), -8.0, 8.0)
    value_values = jnp.clip(jax.random.normal(value_base, full_shape, jnp.float32), -6.0, 6.0)
    return jnp.stack([key_values, value_values], axis=2).astype(jnp.bfloat16)


def draw_head_reach(key, part):
    columns = []
    for column in range(2):
        shuffled = jax.random.permutation(jax.random.fold_in(key, 20 + column), HEADS)
        columns.append((shuffled < 2 * HEADS // 3).astype(jnp.int32))
    return jnp.stack(columns, axis=1)


def draw_tile_extent(key, part):
    frame_counts = jnp.full((TILES_T, TILES_H), TILE_F, jnp.int32)
    frame_edge = jax.random.randint(jax.random.fold_in(key, 30), (TILES_H,), 1, TILE_F, dtype=jnp.int32)
    frame_spot = jax.random.randint(jax.random.fold_in(key, 32), (), 0, TILES_H, dtype=jnp.int32)
    frame_edge = jnp.where(jnp.arange(TILES_H, dtype=jnp.int32) == frame_spot, 1, frame_edge)
    frame_counts = frame_counts.at[TILES_T - 1].set(frame_edge)
    row_counts = jnp.full((TILES_T, TILES_H), TILE_R, jnp.int32)
    row_edge = jax.random.randint(jax.random.fold_in(key, 31), (TILES_T,), 1, TILE_R, dtype=jnp.int32)
    row_spot = jax.random.randint(jax.random.fold_in(key, 33), (), 0, TILES_T, dtype=jnp.int32)
    row_edge = jnp.where(jnp.arange(TILES_T, dtype=jnp.int32) == row_spot, 1, row_edge)
    row_counts = row_counts.at[:, TILES_H - 1].set(row_edge)
    return jnp.stack([frame_counts, row_counts], axis=0)


def level_of(stream_key, extent, split, low, high):
    gain, own = 1.0, jax.random.fold_in(stream_key, 6)
    for dim, shards_of in split:
        draws = jnp.exp(jax.random.uniform(jax.random.fold_in(own, dim), (shards_of,), jnp.float32, low / len(split), high / len(split)))
        gain = gain * jnp.repeat(draws, extent[dim] // shards_of).reshape([-1 if axis == dim else 1 for axis in range(len(extent))])
    return gain


def bell_draw(stream_key, extent, scale, limit, pieces=(), kind=jnp.bfloat16):
    level = level_of(stream_key, extent, pieces, -0.22, 0.18) if pieces else 1.0
    values = jax.random.normal(stream_key, extent, jnp.float32) * scale * level
    return jnp.minimum(jnp.maximum(values, -limit), limit).astype(kind)


def setup_inputs(seed: int = 0) -> dict:
    keys = jax.random.split(jax.random.key(seed), 9)
    return {
        "image_q": draw_image_q(jax.random.fold_in(keys[8], 71), 0),
        "image_kv": draw_image_kv(jax.random.fold_in(keys[8], 71), 0),
        "text_kv": bell_draw(keys[2], (2, TXT, HEADS * HD), 1.8, 8.0, ((1, 2), (2, 4))),
        "residual": bell_draw(keys[3], (TILES_T, TILES_H, TILE, D), 0.5, 3.0, ((0, 2), (1, 4), (3, 4))),
        "out_weight": bell_draw(keys[4], (HEADS * HD, D), (HEADS * HD) ** -0.5, 0.109375, ((0, 4),)),
        "out_gate": jnp.clip(0.5 + 1.5 * jax.random.uniform(keys[5], (D,), jnp.float32) ** level_of(keys[5], (D,), ((0, 4),), -0.2, 0.2), 0.5, 2.0),
        "head_reach": draw_head_reach(jax.random.fold_in(keys[8], 71), 0),
        "tile_extent": draw_tile_extent(jax.random.fold_in(keys[8], 71), 0),
    }


def token_masks(extent_pair):
    positions = jnp.arange(TILE_F * TILE_R * TILE_C, dtype=jnp.int32)
    frame_of = positions // (TILE_R * TILE_C)
    row_of = positions // TILE_C % TILE_R
    frame_ok = frame_of < extent_pair[0][..., None]
    row_ok = row_of < extent_pair[1][..., None]
    return jnp.logical_and(frame_ok, row_ok)

def reference(image_q, image_kv, text_kv, residual, out_weight, out_gate, head_reach, tile_extent):
    tiles_time = image_q.shape[0]
    tiles_height = image_q.shape[1]
    tile_len = image_q.shape[2]
    col_width = image_q.shape[3]
    head_count = col_width // HD
    model_width = residual.shape[3]
    padded_kv = jnp.pad(image_kv, ((1, 1), (1, 1), (0, 0), (0, 0), (0, 0)))
    padded_ext = jnp.pad(tile_extent, ((0, 0), (1, 1), (1, 1)))
    key_valid = token_masks(padded_ext)
    query_valid = token_masks(tile_extent).reshape(-1, tile_len)
    flat_q = image_q.reshape(-1, tile_len, col_width)
    offsets = jnp.abs(jnp.arange(3, dtype=jnp.int32) - 1)
    scale_factor = 1.0 / math.sqrt(HD)
    text_keys = text_kv[0].astype(jnp.float32).reshape(TXT, head_count, HD)
    text_values = text_kv[1].astype(jnp.float32).reshape(TXT, head_count, HD)
    zero_index = jnp.int32(0)
    reach_time = head_reach[:, 0]
    reach_height = head_reach[:, 1]

    def one_tile(tile_index):
        time_tile = tile_index // tiles_height
        height_tile = tile_index % tiles_height
        window = lax.dynamic_slice(padded_kv, (time_tile, height_tile, zero_index, zero_index, zero_index), (3, 3, 2, tile_len, col_width))
        key_ok = lax.dynamic_slice(key_valid, (time_tile, height_tile, zero_index), (3, 3, tile_len))
        key_rows = jnp.concatenate([window[:, :, 0].astype(jnp.float32).reshape(-1, head_count, HD), text_keys], axis=0)
        value_rows = jnp.concatenate([window[:, :, 1].astype(jnp.float32).reshape(-1, head_count, HD), text_values], axis=0)
        image_ok = key_ok[None]
        image_ok = jnp.logical_and(image_ok, offsets[None, :, None, None] <= reach_time[:, None, None, None])
        image_ok = jnp.logical_and(image_ok, offsets[None, None, :, None] <= reach_height[:, None, None, None])
        allowed = jnp.concatenate([image_ok.reshape(head_count, -1), jnp.ones((head_count, TXT), jnp.bool_)], axis=1)
        query_f32 = flat_q[tile_index].astype(jnp.float32).reshape(tile_len, head_count, HD)
        scores = jnp.einsum('ind,jnd->nij', query_f32, key_rows) * scale_factor
        masked = jnp.where(allowed[:, None, :], scores, -1e+30)
        top_score = lax.optimization_barrier(jnp.max(masked, axis=2, keepdims=True))
        weights = jnp.where(allowed[:, None, :], jnp.exp(masked - top_score), 0.0)
        row_total = lax.optimization_barrier(jnp.sum(weights, axis=2))
        rounded = lax.optimization_barrier(weights.astype(jnp.bfloat16)).astype(jnp.float32)
        attended = jnp.einsum('nij,jnd->ind', rounded, value_rows) / jnp.transpose(row_total)[:, :, None]
        attended = jnp.where(query_valid[tile_index][:, None, None], attended, 0.0)
        return attended.reshape(tile_len, col_width).astype(jnp.bfloat16)
    attended = lax.map(one_tile, jnp.arange(flat_q.shape[0], dtype=jnp.int32))
    flat_rows = attended.reshape(-1, col_width)
    group_width = col_width // HEAD_GROUPS
    branch = jnp.zeros((flat_rows.shape[0], model_width), jnp.float32)
    for group_index in range(HEAD_GROUPS):
        low_col = group_index * group_width
        part_sum = jnp.dot(flat_rows[:, low_col:low_col + group_width], out_weight[low_col:low_col + group_width], preferred_element_type=jnp.float32).astype(jnp.bfloat16)
        branch = branch + lax.optimization_barrier(part_sum).astype(jnp.float32)
    updated = residual.astype(jnp.float32).reshape(-1, model_width) + out_gate[None, :] * branch
    return updated.astype(jnp.bfloat16).reshape(residual.shape)
```

```python
import functools
import math

import jax
import jax.numpy as jnp
from jax import lax
from jax.experimental import pallas as pl
from jax.experimental.pallas import tpu as pltpu
from jax.sharding import PartitionSpec as P

HD = 128
TILE_F = 6
TILE_R = 8
TILE_C = 8
HEADS_PER_CHUNK = 2
ROW_CHUNKS = 3
NEG = -1e30
MESH = pl.DeviceIdType.MESH


def kernel(
    sizes,
    q_ref, kv_hbm, text_hbm, res_hbm, w_hbm, gate_ref, reach_ref, extent_ref,
    out_ref,
    buf, txt, w_ref, res_ref, att, acc, top, total, final,
    right_out, right_in, left_out, left_in,
    local_sem, text_send, text_recv, text_fsend, text_frecv,
    time_send, high_send, kv_recv,
    right_send, right_recv, left_send, left_recv,
):
    tm, height, mp, slots = sizes
    tile, width = q_ref.shape
    heads = width // HD
    chunks = heads // HEADS_PER_CHUNK
    chunk_width = HEADS_PER_CHUNK * HD
    text_rows = text_hbm.shape[1]
    t, h, m = lax.axis_index("tm"), lax.axis_index("height"), lax.axis_index("mp")
    scale = math.log2(math.e) / math.sqrt(HD)

    if tm == 1:
        times = []
    elif tm == 2:
        times = [(1, 1 - t, t >= 0, 1)]
    else:
        times = [(1, t - 1, t > 0, 2), (2, t + 1, t < tm - 1, 1)]
    highs = [(0, h - 1, h > 0, 2), (2, h + 1, h < height - 1, 0)]
    pair = h + 1 - 2 * (h % 2)
    parity = h % 2

    own_kv = pltpu.make_async_copy(kv_hbm, buf.at[0, 1], local_sem.at[0])
    own_rows = pl.ds(pl.multiple_of(t * text_rows, text_rows), text_rows)
    own_text = pltpu.make_async_copy(text_hbm, txt.at[:, own_rows], local_sem.at[1])
    w_copy = pltpu.make_async_copy(w_hbm, w_ref, local_sem.at[2])
    res_copy = pltpu.make_async_copy(res_hbm, res_ref, local_sem.at[3])
    own_kv.start()
    own_text.start()

    barrier = pltpu.get_barrier_semaphore()
    for step in range(1, tm):
        pl.semaphore_signal(
            barrier, inc=1, device_id={"tm": (t + step) % tm}, device_id_type=MESH
        )
    line = [("height", h - 1, h > 0), ("height", h + 1, h < height - 1),
            ("mp", m - 1, m > 0), ("mp", m + 1, m < mp - 1)]
    for axis, peer, there in line:
        @pl.when(there)
        def _(axis=axis, peer=peer):
            pl.semaphore_signal(
                barrier, inc=1, device_id={axis: peer}, device_id_type=MESH
            )
    count = tm - 1
    for _, _, there in line:
        count = count + there.astype(jnp.int32)
    pl.semaphore_wait(barrier, count)

    def cols_of(c):
        return pl.ds(c * chunk_width, chunk_width)

    def text_copy(step):
        peer = (t + step) % tm
        return pltpu.make_async_remote_copy(
            src_ref=text_hbm.at[parity],
            dst_ref=txt.at[parity, own_rows],
            send_sem=text_send.at[step], recv_sem=text_recv.at[step],
            device_id={"tm": peer}, device_id_type=MESH,
        )

    def text_arrived(step, kind):
        rows = pl.ds(pl.multiple_of(((t + tm - step) % tm) * text_rows, text_rows), text_rows)
        return txt.at[kind, rows]

    def text_landed(step):
        ref = text_arrived(step, parity)
        return pltpu.make_async_remote_copy(
            src_ref=ref, dst_ref=ref,
            send_sem=text_send.at[step], recv_sem=text_recv.at[step],
            device_id={"tm": (t + step) % tm}, device_id_type=MESH,
        )

    def text_forward(step, kind):
        ref = text_arrived(step, kind)
        return pltpu.make_async_remote_copy(
            src_ref=ref, dst_ref=ref,
            send_sem=text_fsend.at[step], recv_sem=text_frecv.at[step],
            device_id={"height": pair}, device_id_type=MESH,
        )

    def time_copy(c, slot, peer, there_slot):
        return pltpu.make_async_remote_copy(
            src_ref=kv_hbm.at[:, :, cols_of(c)],
            dst_ref=buf.at[there_slot, 1, :, :, cols_of(c)],
            send_sem=time_send.at[slot, c], recv_sem=kv_recv.at[there_slot, 1, c],
            device_id={"tm": peer}, device_id_type=MESH,
        )

    def high_copy(c, slot, side, peer, there_side):
        src = kv_hbm if slot == 0 else buf.at[slot, 1]
        return pltpu.make_async_remote_copy(
            src_ref=src.at[:, :, cols_of(c)],
            dst_ref=buf.at[slot, there_side, :, :, cols_of(c)],
            send_sem=high_send.at[slot, side, c],
            recv_sem=kv_recv.at[slot, there_side, c],
            device_id={"height": peer}, device_id_type=MESH,
        )

    def wait_landed(c, slot, side, axis, peer):
        ref = buf.at[slot, side, :, :, cols_of(c)]
        pltpu.make_async_remote_copy(
            src_ref=ref, dst_ref=ref,
            send_sem=high_send.at[slot, 0, c], recv_sem=kv_recv.at[slot, side, c],
            device_id={axis: peer}, device_id_type=MESH,
        ).wait_recv()

    for step in range(1, tm):
        text_copy(step).start()
    for c in range(chunks):
        for slot, peer, there, there_slot in times:
            @pl.when(there)
            def _(c=c, slot=slot, peer=peer, there_slot=there_slot):
                time_copy(c, slot, peer, there_slot).start()
        for side, peer, there, there_side in highs:
            @pl.when(there)
            def _(c=c, side=side, peer=peer, there_side=there_side):
                high_copy(c, 0, side, peer, there_side).start()
    w_copy.start()
    res_copy.start()

    position = lax.broadcasted_iota(jnp.int32, (1, tile), 1)
    frame_of = position // (TILE_R * TILE_C)
    row_of = position // TILE_C % TILE_R

    def bias_of(head, slot, side):
        dt = 0 if slot == 0 else 1
        dh = 0 if side == 1 else 1
        if slot == 0:
            t2 = t
        elif tm == 2:
            t2 = 1 - t
        else:
            t2 = t + (2 * slot - 3)
        h2 = h + side - 1
        frames = extent_ref[0, t2, h2]
        rows = extent_ref[1, t2, h2]
        near = jnp.logical_and(reach_ref[head, 0] >= dt, reach_ref[head, 1] >= dh)
        frames = jnp.where(near, frames, 0)
        ok = jnp.logical_and(frame_of < frames, row_of < rows)
        return jnp.where(ok, 0.0, NEG)

    def piece(head, k_of, v_of, bias, first=False):
        cols = pl.ds(pl.multiple_of(head * HD, HD), HD)
        s = lax.dot_general(
            q_ref[:, cols], k_of(cols), (((1,), (1,)), ((), ())),
            preferred_element_type=jnp.float32,
        ) * scale
        if bias is not None:
            s = s + bias
        peak = jnp.max(s, axis=1, keepdims=True)
        if not first:
            old = top[head]
            peak = jnp.maximum(peak, old)
        p = jnp.exp2(s - peak)
        row_sum = jnp.sum(p, axis=1, keepdims=True)
        pv = jnp.dot(p.astype(jnp.bfloat16), v_of(cols), preferred_element_type=jnp.float32)
        if not first:
            alpha = jnp.exp2(old - peak)
            row_sum = row_sum + alpha * total[head]
            pv = pv + alpha * acc[head]
        top[head] = peak
        total[head] = row_sum
        acc[head] = pv

    def image_piece(head, slot, side, first=False):
        piece(
            head,
            lambda cols: buf[slot, side, 0, :, cols],
            lambda cols: buf[slot, side, 1, :, cols],
            bias_of(head, slot, side), first,
        )

    own_kv.wait()

    @pl.loop(0, heads)
    def _(head):
        image_piece(head, 0, 1, True)

    for step in range(1, tm):
        text_landed(step).wait_recv()
        text_forward(step, parity).start()
    own_text.wait()
    for step in range(1, tm):
        text_forward(step, 1 - parity).wait_recv()

    @pl.loop(0, heads)
    def _(head):
        piece(head, lambda cols: txt[0, :, cols], lambda cols: txt[1, :, cols], None)

    def heads_of(c, slot, side):
        @pl.loop(c * HEADS_PER_CHUNK, (c + 1) * HEADS_PER_CHUNK)
        def _(head):
            image_piece(head, slot, side)

    query = lax.broadcasted_iota(jnp.int32, (tile, 1), 0)
    query_ok = jnp.logical_and(
        query // (TILE_R * TILE_C) < extent_ref[0, t, h],
        query // TILE_C % TILE_R < extent_ref[1, t, h],
    )

    def corners(c):
        for slot, _, there, _ in times:
            for side, peer, near, _ in highs:
                @pl.when(jnp.logical_and(there, near))
                def _(slot=slot, side=side, peer=peer):
                    wait_landed(c, slot, side, "height", peer)
                    heads_of(c, slot, side)

        @pl.loop(c * HEADS_PER_CHUNK, (c + 1) * HEADS_PER_CHUNK)
        def _(head):
            value = jnp.where(query_ok, acc[head] / total[head], 0.0)
            cols = pl.ds(pl.multiple_of(head * HD, HD), HD)
            att[:, cols] = value.astype(jnp.bfloat16)

    for c in range(chunks):
        for side, peer, there, _ in highs:
            @pl.when(there)
            def _(c=c, side=side, peer=peer):
                wait_landed(c, 0, side, "height", peer)
                heads_of(c, 0, side)
        for slot, peer, there, _ in times:
            @pl.when(there)
            def _(c=c, slot=slot, peer=peer):
                wait_landed(c, slot, 1, "tm", peer)
                for side, high_peer, near, there_side in highs:
                    @pl.when(near)
                    def _(side=side, high_peer=high_peer, there_side=there_side):
                        high_copy(c, slot, side, high_peer, there_side).start()
                heads_of(c, slot, 1)
        if c > 0:
            corners(c - 1)
    corners(chunks - 1)

    w_copy.wait()
    step_rows = tile // ROW_CHUNKS
    block = w_ref.shape[1] // mp

    def rows_of(r):
        return pl.ds(pl.multiple_of(r * step_rows, step_rows), step_rows)

    def part(d, r):
        if isinstance(d, int):
            columns = pl.ds(d * block, block)
        else:
            columns = pl.ds(pl.multiple_of(d * block, block), block)
        return jnp.dot(att[rows_of(r), :], w_ref[:, columns], preferred_element_type=jnp.float32)

    def right_copy(d, r):
        return pltpu.make_async_remote_copy(
            src_ref=right_out.at[d, rows_of(r)], dst_ref=right_in.at[d, rows_of(r)],
            send_sem=right_send.at[d, r], recv_sem=right_recv.at[d, r],
            device_id={"mp": m + 1}, device_id_type=MESH,
        )

    def left_copy(d, r):
        return pltpu.make_async_remote_copy(
            src_ref=left_out.at[d, rows_of(r)], dst_ref=left_in.at[d, rows_of(r)],
            send_sem=left_send.at[d, r], recv_sem=left_recv.at[d, r],
            device_id={"mp": m - 1}, device_id_type=MESH,
        )

    for k in range(mp - 1):
        @pl.loop(0, ROW_CHUNKS)
        def _(r, k=k):
            d = mp - 1 - k
            for dest, sends, inner, out, arrived, copy in (
                (d, m < d, m > 0, right_out, right_in, right_copy),
                (k, m > k, m < mp - 1, left_out, left_in, left_copy),
            ):
                @pl.when(jnp.logical_and(sends, jnp.logical_not(inner)))
                def _(dest=dest, out=out, copy=copy):
                    out[dest, rows_of(r), :] = part(dest, r).astype(jnp.bfloat16)
                    copy(dest, r).start()

                @pl.when(jnp.logical_and(sends, inner))
                def _(dest=dest, out=out, arrived=arrived, copy=copy):
                    value = part(dest, r)
                    copy(dest, r).wait_recv()
                    value = value + arrived[dest, rows_of(r), :].astype(jnp.float32)
                    out[dest, rows_of(r), :] = value.astype(jnp.bfloat16)
                    copy(dest, r).start()

    res_copy.wait()

    @pl.loop(0, ROW_CHUNKS)
    def _(r):
        final[...] = part(m, r)
        for arrived, sem, side, there in (
            (right_in, right_recv, -1, m > 0), (left_in, left_recv, 1, m < mp - 1)
        ):
            @pl.when(there)
            def _(arrived=arrived, sem=sem, side=side):
                ref = arrived.at[m, rows_of(r)]
                pltpu.make_async_remote_copy(
                    src_ref=ref, dst_ref=ref,
                    send_sem=local_sem.at[0], recv_sem=sem.at[m, r],
                    device_id={"mp": m + side}, device_id_type=MESH,
                ).wait_recv()
                final[...] += arrived[m, rows_of(r), :].astype(jnp.float32)
        value = res_ref[rows_of(r), :].astype(jnp.float32) + gate_ref[...] * final[...]
        out_ref[rows_of(r), :] = value.astype(jnp.bfloat16)

    for step in range(1, tm):
        text_copy(step).wait_send()
        text_forward(step, parity).wait_send()
    for c in range(chunks):
        for slot, peer, there, there_slot in times:
            @pl.when(there)
            def _(c=c, slot=slot, peer=peer, there_slot=there_slot):
                time_copy(c, slot, peer, there_slot).wait_send()
        for side, peer, near, there_side in highs:
            @pl.when(near)
            def _(c=c, side=side, peer=peer, there_side=there_side):
                high_copy(c, 0, side, peer, there_side).wait_send()
                for slot, _, there, _ in times:
                    @pl.when(there)
                    def _(slot=slot):
                        high_copy(c, slot, side, peer, there_side).wait_send()
    for k in range(mp - 1):
        @pl.loop(0, ROW_CHUNKS)
        def _(r, k=k):
            @pl.when(m < mp - 1 - k)
            def _():
                right_copy(mp - 1 - k, r).wait_send()

            @pl.when(m > k)
            def _():
                left_copy(k, r).wait_send()


def per_device(image_q, image_kv, text_kv, residual, out_weight, out_gate, head_reach, tile_extent):
    tm, height, mp = (lax.axis_size(axis) for axis in ("tm", "height", "mp"))
    tile, width = image_q.shape[2:]
    heads = width // HD
    chunks = heads // HEADS_PER_CHUNK
    slots = min(tm, 3)
    block = residual.shape[3]
    text = text_kv.shape[1] * tm
    half = jnp.bfloat16
    dma = pltpu.SemaphoreType.DMA
    vmem = pl.BlockSpec(memory_space=pltpu.VMEM)
    smem = pl.BlockSpec(memory_space=pltpu.SMEM)
    anywhere = pl.BlockSpec(memory_space=pl.ANY)
    result = pl.pallas_call(
        functools.partial(kernel, (tm, height, mp, slots)),
        out_shape=jax.ShapeDtypeStruct((tile, block), half),
        in_specs=[vmem, anywhere, anywhere, anywhere, anywhere, vmem, smem, smem],
        out_specs=vmem,
        scratch_shapes=[
            pltpu.VMEM((slots, 3, 2, tile, width), half),
            pltpu.VMEM((2, text, width), half),
            pltpu.VMEM(out_weight.shape, half),
            pltpu.VMEM((tile, block), half),
            pltpu.VMEM((tile, width), half),
            pltpu.VMEM((heads, tile, HD), jnp.float32),
            pltpu.VMEM((heads, tile, 1), jnp.float32),
            pltpu.VMEM((heads, tile, 1), jnp.float32),
            pltpu.VMEM((tile // ROW_CHUNKS, block), jnp.float32),
        ]
        + [pltpu.VMEM((mp, tile, block), half)] * 4
        + [
            dma((4,)), dma((tm,)), dma((tm,)), dma((tm,)), dma((tm,)),
            dma((slots, chunks)), dma((slots, 3, chunks)), dma((slots, 3, chunks)),
        ]
        + [dma((mp, ROW_CHUNKS))] * 4,
        compiler_params=pltpu.CompilerParams(
            collective_id=0, has_side_effects=True, vmem_limit_bytes=56 * 2**20
        ),
        cost_estimate=pl.CostEstimate(
            flops=6 * 10**9, bytes_accessed=8 * 10**6, transcendentals=6 * 10**6
        ),
    )(
        image_q.reshape(tile, width),
        image_kv.reshape(2, tile, width),
        text_kv,
        residual.reshape(tile, block),
        out_weight,
        out_gate.reshape(1, block),
        head_reach,
        tile_extent,
    )
    return result.reshape(residual.shape)


def solution(mesh):
    return jax.shard_map(
        per_device,
        mesh=mesh,
        in_specs=(
            P("tm", "height", None, "mp"),
            P("tm", "height", None, None, "mp"),
            P(None, "tm", "mp"),
            P("tm", "height", None, "mp"),
            P("mp", None),
            P("mp"),
            P("mp", None),
            P(),
        ),
        out_specs=P("tm", "height", None, "mp"),
        check_vma=False,
    )
```

```python
import functools
import math

import jax
import jax.numpy as jnp
from jax import lax
from jax.experimental import pallas as pl
from jax.experimental.pallas import tpu as pltpu
from jax.sharding import PartitionSpec as P

HD = 128
TILE_F = 6
TILE_R = 8
TILE_C = 8
HEADS_PER_CHUNK = 1
ROW_CHUNKS = 3
LEAD = 2
NEG = -1e30
MESH = pl.DeviceIdType.MESH


def kernel(
    sizes,
    q_ref, kv_hbm, text_hbm, res_hbm, w_hbm, gate_ref, reach_ref, extent_ref,
    out_ref,
    buf, txt, w_ref, res_ref, att, acc, top, total, final,
    right_out, right_in, left_out, left_in,
    local_sem, text_send, text_recv, text_fsend, text_frecv,
    time_send, high_send, kv_recv,
    right_send, right_recv, left_send, left_recv,
):
    tm, height, mp, slots = sizes
    tile, width = q_ref.shape
    heads = width // HD
    chunks = heads // HEADS_PER_CHUNK
    chunk_width = HEADS_PER_CHUNK * HD
    text_rows = text_hbm.shape[1]
    t, h, m = lax.axis_index("tm"), lax.axis_index("height"), lax.axis_index("mp")
    scale = math.log2(math.e) / math.sqrt(HD)

    if tm == 1:
        times = []
    elif tm == 2:
        times = [(1, 1 - t, t >= 0, 1)]
    else:
        times = [(1, t - 1, t > 0, 2), (2, t + 1, t < tm - 1, 1)]
    highs = [(0, h - 1, h > 0, 2), (2, h + 1, h < height - 1, 0)]
    pair = h + 1 - 2 * (h % 2)
    parity = h % 2

    own_kv = pltpu.make_async_copy(kv_hbm, buf.at[0, 1], local_sem.at[0])
    own_rows = pl.ds(pl.multiple_of(t * text_rows, text_rows), text_rows)
    own_text = pltpu.make_async_copy(text_hbm, txt.at[:, own_rows], local_sem.at[1])
    w_copy = pltpu.make_async_copy(w_hbm, w_ref, local_sem.at[2])
    res_copy = pltpu.make_async_copy(res_hbm, res_ref, local_sem.at[3])
    own_kv.start()
    own_text.start()

    barrier = pltpu.get_barrier_semaphore()
    for step in range(1, tm):
        pl.semaphore_signal(
            barrier, inc=1, device_id={"tm": (t + step) % tm}, device_id_type=MESH
        )
    line = [("height", h - 1, h > 0), ("height", h + 1, h < height - 1),
            ("mp", m - 1, m > 0), ("mp", m + 1, m < mp - 1)]
    for axis, peer, there in line:
        @pl.when(there)
        def _(axis=axis, peer=peer):
            pl.semaphore_signal(
                barrier, inc=1, device_id={axis: peer}, device_id_type=MESH
            )
    count = tm - 1
    for _, _, there in line:
        count = count + there.astype(jnp.int32)
    pl.semaphore_wait(barrier, count)

    def cols_of(c):
        return pl.ds(c * chunk_width, chunk_width)

    def text_copy(step):
        peer = (t + step) % tm
        return pltpu.make_async_remote_copy(
            src_ref=text_hbm.at[parity],
            dst_ref=txt.at[parity, own_rows],
            send_sem=text_send.at[step], recv_sem=text_recv.at[step],
            device_id={"tm": peer}, device_id_type=MESH,
        )

    def text_arrived(step, kind):
        rows = pl.ds(pl.multiple_of(((t + tm - step) % tm) * text_rows, text_rows), text_rows)
        return txt.at[kind, rows]

    def text_landed(step):
        ref = text_arrived(step, parity)
        return pltpu.make_async_remote_copy(
            src_ref=ref, dst_ref=ref,
            send_sem=text_send.at[step], recv_sem=text_recv.at[step],
            device_id={"tm": (t + step) % tm}, device_id_type=MESH,
        )

    def text_forward(step, kind):
        ref = text_arrived(step, kind)
        return pltpu.make_async_remote_copy(
            src_ref=ref, dst_ref=ref,
            send_sem=text_fsend.at[step], recv_sem=text_frecv.at[step],
            device_id={"height": pair}, device_id_type=MESH,
        )

    def time_copy(c, slot, peer, there_slot):
        return pltpu.make_async_remote_copy(
            src_ref=kv_hbm.at[:, :, cols_of(c)],
            dst_ref=buf.at[there_slot, 1, :, :, cols_of(c)],
            send_sem=time_send.at[slot, c], recv_sem=kv_recv.at[there_slot, 1, c],
            device_id={"tm": peer}, device_id_type=MESH,
        )

    def high_copy(c, slot, side, peer, there_side):
        src = kv_hbm if slot == 0 else buf.at[slot, 1]
        return pltpu.make_async_remote_copy(
            src_ref=src.at[:, :, cols_of(c)],
            dst_ref=buf.at[slot, there_side, :, :, cols_of(c)],
            send_sem=high_send.at[slot, side, c],
            recv_sem=kv_recv.at[slot, there_side, c],
            device_id={"height": peer}, device_id_type=MESH,
        )

    def wait_landed(c, slot, side, axis, peer):
        ref = buf.at[slot, side, :, :, cols_of(c)]
        pltpu.make_async_remote_copy(
            src_ref=ref, dst_ref=ref,
            send_sem=high_send.at[slot, 0, c], recv_sem=kv_recv.at[slot, side, c],
            device_id={axis: peer}, device_id_type=MESH,
        ).wait_recv()

    for step in range(1, tm):
        text_copy(step).start()
    for c in range(chunks):
        for slot, peer, there, there_slot in times:
            @pl.when(there)
            def _(c=c, slot=slot, peer=peer, there_slot=there_slot):
                time_copy(c, slot, peer, there_slot).start()
        for side, peer, there, there_side in highs:
            @pl.when(there)
            def _(c=c, side=side, peer=peer, there_side=there_side):
                high_copy(c, 0, side, peer, there_side).start()
    w_copy.start()
    res_copy.start()

    position = lax.broadcasted_iota(jnp.int32, (1, tile), 1)
    frame_of = position // (TILE_R * TILE_C)
    row_of = position // TILE_C % TILE_R

    def bias_of(head, slot, side):
        dt = 0 if slot == 0 else 1
        dh = 0 if side == 1 else 1
        if slot == 0:
            t2 = t
        elif tm == 2:
            t2 = 1 - t
        else:
            t2 = t + (2 * slot - 3)
        h2 = h + side - 1
        frames = extent_ref[0, t2, h2]
        rows = extent_ref[1, t2, h2]
        near = jnp.logical_and(reach_ref[0, head] >= dt, reach_ref[1, head] >= dh)
        frames = jnp.where(near, frames, 0)
        ok = jnp.logical_and(frame_of < frames, row_of < rows)
        return jnp.where(ok, 0.0, NEG)

    def piece(head, k_of, v_of, bias, first=False):
        cols = pl.ds(pl.multiple_of(head * HD, HD), HD)
        s = lax.dot_general(
            q_ref[:, cols], k_of(cols), (((1,), (1,)), ((), ())),
            preferred_element_type=jnp.float32,
        ) * scale
        if bias is not None:
            s = s + bias
        peak = jnp.max(s, axis=1, keepdims=True)
        if not first:
            old = top[head]
            peak = jnp.maximum(peak, old)
        p = jnp.exp2(s - peak)
        row_sum = jnp.sum(p, axis=1, keepdims=True)
        pv = jnp.dot(p.astype(jnp.bfloat16), v_of(cols), preferred_element_type=jnp.float32)
        if not first:
            alpha = jnp.exp2(old - peak)
            row_sum = row_sum + alpha * total[head]
            pv = pv + alpha * acc[head]
        top[head] = peak
        total[head] = row_sum
        acc[head] = pv

    def image_piece(head, slot, side, first=False):
        piece(
            head,
            lambda cols: buf[slot, side, 0, :, cols],
            lambda cols: buf[slot, side, 1, :, cols],
            bias_of(head, slot, side), first,
        )

    own_kv.wait()

    @pl.loop(0, heads)
    def _(head):
        image_piece(head, 0, 1, True)

    for step in range(1, tm):
        text_landed(step).wait_recv()
        text_forward(step, parity).start()
    own_text.wait()
    for step in range(1, tm):
        text_forward(step, 1 - parity).wait_recv()

    @pl.loop(0, heads)
    def _(head):
        piece(head, lambda cols: txt[0, :, cols], lambda cols: txt[1, :, cols], None)

    def heads_of(c, slot, side):
        @pl.loop(c * HEADS_PER_CHUNK, (c + 1) * HEADS_PER_CHUNK)
        def _(head):
            image_piece(head, slot, side)

    query = lax.broadcasted_iota(jnp.int32, (tile, 1), 0)
    query_ok = jnp.logical_and(
        query // (TILE_R * TILE_C) < extent_ref[0, t, h],
        query // TILE_C % TILE_R < extent_ref[1, t, h],
    )

    def corners(c):
        for slot, _, there, _ in times:
            for side, peer, near, _ in highs:
                @pl.when(jnp.logical_and(there, near))
                def _(slot=slot, side=side, peer=peer):
                    wait_landed(c, slot, side, "height", peer)
                    heads_of(c, slot, side)

        @pl.loop(c * HEADS_PER_CHUNK, (c + 1) * HEADS_PER_CHUNK)
        def _(head):
            value = jnp.where(query_ok, acc[head] / total[head], 0.0)
            cols = pl.ds(pl.multiple_of(head * HD, HD), HD)
            att[:, cols] = value.astype(jnp.bfloat16)

    for c in range(chunks):
        for side, peer, there, _ in highs:
            @pl.when(there)
            def _(c=c, side=side, peer=peer):
                wait_landed(c, 0, side, "height", peer)
                heads_of(c, 0, side)
        for slot, peer, there, _ in times:
            @pl.when(there)
            def _(c=c, slot=slot, peer=peer):
                wait_landed(c, slot, 1, "tm", peer)
                for side, high_peer, near, there_side in highs:
                    @pl.when(near)
                    def _(side=side, high_peer=high_peer, there_side=there_side):
                        high_copy(c, slot, side, high_peer, there_side).start()
                heads_of(c, slot, 1)
        if c > 0:
            corners(c - 1)
    corners(chunks - 1)

    w_copy.wait()
    step_rows = tile // ROW_CHUNKS
    block = w_ref.shape[1] // mp

    def rows_of(r):
        return pl.ds(pl.multiple_of(r * step_rows, step_rows), step_rows)

    def part(d, r):
        if isinstance(d, int):
            columns = pl.ds(d * block, block)
        else:
            columns = pl.ds(pl.multiple_of(d * block, block), block)
        return jnp.dot(att[rows_of(r), :], w_ref[:, columns], preferred_element_type=jnp.float32)

    def right_copy(d, r):
        return pltpu.make_async_remote_copy(
            src_ref=right_out.at[d, rows_of(r)], dst_ref=right_in.at[d, rows_of(r)],
            send_sem=right_send.at[d, r], recv_sem=right_recv.at[d, r],
            device_id={"mp": m + 1}, device_id_type=MESH,
        )

    def left_copy(d, r):
        return pltpu.make_async_remote_copy(
            src_ref=left_out.at[d, rows_of(r)], dst_ref=left_in.at[d, rows_of(r)],
            send_sem=left_send.at[d, r], recv_sem=left_recv.at[d, r],
            device_id={"mp": m - 1}, device_id_type=MESH,
        )

    def stream_step(step, to_right):
        k, r = step // ROW_CHUNKS, step % ROW_CHUNKS
        if to_right:
            d, out, arrived, copy = mp - 1 - k, right_out, right_in, right_copy
            sends, inner = m < d, m > 0
        else:
            d, out, arrived, copy = k, left_out, left_in, left_copy
            sends, inner = m > d, m < mp - 1

        @pl.when(sends)
        def _():
            final[...] = part(d, r)

            @pl.when(inner)
            def _():
                copy(d, r).wait_recv()
                final[...] += arrived[d, rows_of(r), :].astype(jnp.float32)

            out[d, rows_of(r), :] = final[...].astype(jnp.bfloat16)
            copy(d, r).start()

    steps = (mp - 1) * ROW_CHUNKS
    for near, right_first in ((m < mp // 2, True), (m >= mp // 2, False)):
        @pl.when(near)
        def _(right_first=right_first):
            @pl.loop(0, steps + LEAD)
            def _(step):
                @pl.when(step < steps)
                def _():
                    stream_step(step, right_first)

                @pl.when(step >= LEAD)
                def _():
                    stream_step(step - LEAD, not right_first)

    res_copy.wait()

    @pl.loop(0, ROW_CHUNKS)
    def _(r):
        final[...] = part(m, r)
        for arrived, sem, side, there in (
            (right_in, right_recv, -1, m > 0), (left_in, left_recv, 1, m < mp - 1)
        ):
            @pl.when(there)
            def _(arrived=arrived, sem=sem, side=side):
                ref = arrived.at[m, rows_of(r)]
                pltpu.make_async_remote_copy(
                    src_ref=ref, dst_ref=ref,
                    send_sem=local_sem.at[0], recv_sem=sem.at[m, r],
                    device_id={"mp": m + side}, device_id_type=MESH,
                ).wait_recv()
                final[...] += arrived[m, rows_of(r), :].astype(jnp.float32)
        value = res_ref[rows_of(r), :].astype(jnp.float32) + gate_ref[...][None, :] * final[...]
        out_ref[rows_of(r), :] = value.astype(jnp.bfloat16)

    for step in range(1, tm):
        text_copy(step).wait_send()
        text_forward(step, parity).wait_send()
    for c in range(chunks):
        for slot, peer, there, there_slot in times:
            @pl.when(there)
            def _(c=c, slot=slot, peer=peer, there_slot=there_slot):
                time_copy(c, slot, peer, there_slot).wait_send()
        for side, peer, near, there_side in highs:
            @pl.when(near)
            def _(c=c, side=side, peer=peer, there_side=there_side):
                high_copy(c, 0, side, peer, there_side).wait_send()
                for slot, _, there, _ in times:
                    @pl.when(there)
                    def _(slot=slot):
                        high_copy(c, slot, side, peer, there_side).wait_send()
    for k in range(mp - 1):
        @pl.loop(0, ROW_CHUNKS)
        def _(r, k=k):
            @pl.when(m < mp - 1 - k)
            def _():
                right_copy(mp - 1 - k, r).wait_send()

            @pl.when(m > k)
            def _():
                left_copy(k, r).wait_send()


def per_device(image_q, image_kv, text_kv, residual, out_weight, out_gate, head_reach, tile_extent):
    tm, height, mp = (lax.axis_size(axis) for axis in ("tm", "height", "mp"))
    tile, width = image_q.shape[2:]
    heads = width // HD
    chunks = heads // HEADS_PER_CHUNK
    slots = min(tm, 3)
    block = residual.shape[3]
    text = text_kv.shape[1] * tm
    half = jnp.bfloat16
    dma = pltpu.SemaphoreType.DMA
    vmem = pl.BlockSpec(memory_space=pltpu.VMEM)
    smem = pl.BlockSpec(memory_space=pltpu.SMEM)
    anywhere = pl.BlockSpec(memory_space=pl.ANY)
    result = pl.pallas_call(
        functools.partial(kernel, (tm, height, mp, slots)),
        out_shape=jax.ShapeDtypeStruct((tile, block), half),
        in_specs=[vmem, anywhere, anywhere, anywhere, anywhere, vmem, smem, smem],
        out_specs=vmem,
        scratch_shapes=[
            pltpu.VMEM((slots, 3, 2, tile, width), half),
            pltpu.VMEM((2, text, width), half),
            pltpu.VMEM(out_weight.shape, half),
            pltpu.VMEM((tile, block), half),
            pltpu.VMEM((tile, width), half),
            pltpu.VMEM((heads, tile, HD), jnp.float32),
            pltpu.VMEM((heads, tile, 1), jnp.float32),
            pltpu.VMEM((heads, tile, 1), jnp.float32),
            pltpu.VMEM((tile // ROW_CHUNKS, block), jnp.float32),
        ]
        + [pltpu.VMEM((mp, tile, block), half)] * 4
        + [
            dma((4,)), dma((tm,)), dma((tm,)), dma((tm,)), dma((tm,)),
            dma((slots, chunks)), dma((slots, 3, chunks)), dma((slots, 3, chunks)),
        ]
        + [dma((mp, ROW_CHUNKS))] * 4,
        compiler_params=pltpu.CompilerParams(
            collective_id=0, has_side_effects=True, vmem_limit_bytes=56 * 2**20
        ),
        cost_estimate=pl.CostEstimate(
            flops=6 * 10**9, bytes_accessed=8 * 10**6, transcendentals=6 * 10**6
        ),
    )(
        image_q.reshape(tile, width),
        image_kv.reshape(2, tile, width),
        text_kv,
        residual.reshape(tile, block),
        out_weight,
        out_gate,
        head_reach.T,
        tile_extent,
    )
    return result.reshape(residual.shape)


def solution(mesh):
    return jax.shard_map(
        per_device,
        mesh=mesh,
        in_specs=(
            P("tm", "height", None, "mp"),
            P("tm", "height", None, None, "mp"),
            P(None, "tm", "mp"),
            P("tm", "height", None, "mp"),
            P("mp", None),
            P("mp"),
            P("mp", None),
            P(),
        ),
        out_specs=P("tm", "height", None, "mp"),
        check_vma=False,
    )
```

```python
import functools
import math

import jax
import jax.numpy as jnp
from jax import lax
from jax.experimental import pallas as pl
from jax.experimental.pallas import tpu as pltpu
from jax.sharding import PartitionSpec as P

HD = 128
TILE_F = 6
TILE_R = 8
TILE_C = 8
HEADS_PER_CHUNK = 1
ROW_CHUNKS = 6
LEAD = 4
NEG = -1e30
MESH = pl.DeviceIdType.MESH


def kernel(
    sizes,
    q_ref, kv_hbm, text_hbm, res_hbm, w_hbm, gate_ref, reach_ref, extent_ref,
    out_ref,
    buf, txt, w_ref, res_ref, att, acc, top, total, final,
    right_out, right_in, left_out, left_in,
    local_sem, text_send, text_recv, text_fsend, text_frecv,
    time_send, high_send, kv_recv,
    right_send, right_recv, left_send, left_recv,
):
    tm, height, mp, slots = sizes
    tile, width = q_ref.shape
    heads = width // HD
    chunks = heads // HEADS_PER_CHUNK
    chunk_width = HEADS_PER_CHUNK * HD
    text_rows = text_hbm.shape[1]
    t, h, m = lax.axis_index("tm"), lax.axis_index("height"), lax.axis_index("mp")
    scale = math.log2(math.e) / math.sqrt(HD)

    if tm == 1:
        times = []
    elif tm == 2:
        times = [(1, 1 - t, t >= 0, 1)]
    else:
        times = [(1, t - 1, t > 0, 2), (2, t + 1, t < tm - 1, 1)]
    highs = [(0, h - 1, h > 0, 2), (2, h + 1, h < height - 1, 0)]
    pair = h + 1 - 2 * (h % 2)
    parity = h % 2

    short = tile - TILE_R * TILE_C
    last_time = t == tm - 1

    def by_rows(is_short, act):
        @pl.when(is_short)
        def _():
            act(short)

        @pl.when(jnp.logical_not(is_short))
        def _():
            act(tile)

    own_kv = pltpu.make_async_copy(kv_hbm, buf.at[0, 1], local_sem.at[0])
    own_rows = pl.ds(pl.multiple_of(t * text_rows, text_rows), text_rows)
    own_text = pltpu.make_async_copy(text_hbm, txt.at[:, own_rows], local_sem.at[1])
    w_copy = pltpu.make_async_copy(w_hbm, w_ref, local_sem.at[2])
    res_copy = pltpu.make_async_copy(res_hbm, res_ref, local_sem.at[3])
    own_kv.start()
    own_text.start()

    barrier = pltpu.get_barrier_semaphore()
    for step in range(1, tm):
        pl.semaphore_signal(
            barrier, inc=1, device_id={"tm": (t + step) % tm}, device_id_type=MESH
        )
    line = [("height", h - 1, h > 0), ("height", h + 1, h < height - 1),
            ("mp", m - 1, m > 0), ("mp", m + 1, m < mp - 1)]
    for axis, peer, there in line:
        @pl.when(there)
        def _(axis=axis, peer=peer):
            pl.semaphore_signal(
                barrier, inc=1, device_id={axis: peer}, device_id_type=MESH
            )
    count = tm - 1
    for _, _, there in line:
        count = count + there.astype(jnp.int32)
    pl.semaphore_wait(barrier, count)

    def cols_of(c):
        return pl.ds(c * chunk_width, chunk_width)

    def text_copy(step):
        peer = (t + step) % tm
        return pltpu.make_async_remote_copy(
            src_ref=text_hbm.at[parity],
            dst_ref=txt.at[parity, own_rows],
            send_sem=text_send.at[step], recv_sem=text_recv.at[step],
            device_id={"tm": peer}, device_id_type=MESH,
        )

    def text_arrived(step, kind):
        rows = pl.ds(pl.multiple_of(((t + tm - step) % tm) * text_rows, text_rows), text_rows)
        return txt.at[kind, rows]

    def text_landed(step):
        ref = text_arrived(step, parity)
        return pltpu.make_async_remote_copy(
            src_ref=ref, dst_ref=ref,
            send_sem=text_send.at[step], recv_sem=text_recv.at[step],
            device_id={"tm": (t + step) % tm}, device_id_type=MESH,
        )

    def text_forward(step, kind):
        ref = text_arrived(step, kind)
        return pltpu.make_async_remote_copy(
            src_ref=ref, dst_ref=ref,
            send_sem=text_fsend.at[step], recv_sem=text_frecv.at[step],
            device_id={"height": pair}, device_id_type=MESH,
        )

    def time_copy(c, slot, peer, there_slot, rows):
        return pltpu.make_async_remote_copy(
            src_ref=kv_hbm.at[:, pl.ds(0, rows), cols_of(c)],
            dst_ref=buf.at[there_slot, 1, :, pl.ds(0, rows), cols_of(c)],
            send_sem=time_send.at[slot, c], recv_sem=kv_recv.at[there_slot, 1, c],
            device_id={"tm": peer}, device_id_type=MESH,
        )

    def high_copy(c, slot, side, peer, there_side, rows):
        src = kv_hbm if slot == 0 else buf.at[slot, 1]
        return pltpu.make_async_remote_copy(
            src_ref=src.at[:, pl.ds(0, rows), cols_of(c)],
            dst_ref=buf.at[slot, there_side, :, pl.ds(0, rows), cols_of(c)],
            send_sem=high_send.at[slot, side, c],
            recv_sem=kv_recv.at[slot, there_side, c],
            device_id={"height": peer}, device_id_type=MESH,
        )

    def wait_landed(c, slot, side, axis, peer, rows):
        ref = buf.at[slot, side, :, pl.ds(0, rows), cols_of(c)]
        pltpu.make_async_remote_copy(
            src_ref=ref, dst_ref=ref,
            send_sem=high_send.at[slot, 0, c], recv_sem=kv_recv.at[slot, side, c],
            device_id={axis: peer}, device_id_type=MESH,
        ).wait_recv()

    for step in range(1, tm):
        text_copy(step).start()
    for c in range(chunks):
        for slot, peer, there, there_slot in times:
            @pl.when(there)
            def _(c=c, slot=slot, peer=peer, there_slot=there_slot):
                by_rows(
                    last_time, lambda n: time_copy(c, slot, peer, there_slot, n).start()
                )
        for side, peer, there, there_side in highs:
            @pl.when(there)
            def _(c=c, side=side, peer=peer, there_side=there_side):
                high_copy(c, 0, side, peer, there_side, tile).start()
    w_copy.start()
    res_copy.start()
    for slot, peer, there, _ in times:
        @pl.when(jnp.logical_and(there, peer == tm - 1))
        def _(slot=slot):
            for side in range(3):
                buf[slot, side, :, short:, :] = jnp.zeros(
                    (2, tile - short, width), jnp.bfloat16
                )

    position = lax.broadcasted_iota(jnp.int32, (1, tile), 1)
    frame_of = position // (TILE_R * TILE_C)
    row_of = position // TILE_C % TILE_R

    def bias_of(head, slot, side):
        dt = 0 if slot == 0 else 1
        dh = 0 if side == 1 else 1
        if slot == 0:
            t2 = t
        elif tm == 2:
            t2 = 1 - t
        else:
            t2 = t + (2 * slot - 3)
        h2 = h + side - 1
        frames = extent_ref[0, t2, h2]
        rows = extent_ref[1, t2, h2]
        near = jnp.logical_and(reach_ref[0, head] >= dt, reach_ref[1, head] >= dh)
        frames = jnp.where(near, frames, 0)
        ok = jnp.logical_and(frame_of < frames, row_of < rows)
        return jnp.where(ok, 0.0, NEG)

    def piece(head, k_of, v_of, bias, first=False):
        cols = pl.ds(pl.multiple_of(head * HD, HD), HD)
        s = lax.dot_general(
            q_ref[:, cols], k_of(cols), (((1,), (1,)), ((), ())),
            preferred_element_type=jnp.float32,
        ) * scale
        if bias is not None:
            s = s + bias
        peak = jnp.max(s, axis=1, keepdims=True)
        if not first:
            old = top[head]
            peak = jnp.maximum(peak, old)
        p = jnp.exp2(s - peak)
        row_sum = jnp.sum(p, axis=1, keepdims=True)
        pv = jnp.dot(p.astype(jnp.bfloat16), v_of(cols), preferred_element_type=jnp.float32)
        if not first:
            alpha = jnp.exp2(old - peak)
            row_sum = row_sum + alpha * total[head]
            pv = pv + alpha * acc[head]
        top[head] = peak
        total[head] = row_sum
        acc[head] = pv

    def image_piece(head, slot, side, first=False):
        piece(
            head,
            lambda cols: buf[slot, side, 0, :, cols],
            lambda cols: buf[slot, side, 1, :, cols],
            bias_of(head, slot, side), first,
        )

    own_kv.wait()

    @pl.loop(0, heads)
    def _(head):
        image_piece(head, 0, 1, True)

    for step in range(1, tm):
        text_landed(step).wait_recv()
        text_forward(step, parity).start()
    own_text.wait()
    for step in range(1, tm):
        text_forward(step, 1 - parity).wait_recv()

    @pl.loop(0, heads)
    def _(head):
        piece(head, lambda cols: txt[0, :, cols], lambda cols: txt[1, :, cols], None)

    def heads_of(c, slot, side):
        @pl.loop(c * HEADS_PER_CHUNK, (c + 1) * HEADS_PER_CHUNK)
        def _(head):
            image_piece(head, slot, side)

    query = lax.broadcasted_iota(jnp.int32, (tile, 1), 0)
    query_ok = jnp.logical_and(
        query // (TILE_R * TILE_C) < extent_ref[0, t, h],
        query // TILE_C % TILE_R < extent_ref[1, t, h],
    )

    def corners(c):
        for slot, time_peer, there, _ in times:
            for side, peer, near, _ in highs:
                @pl.when(jnp.logical_and(there, near))
                def _(slot=slot, side=side, peer=peer, time_peer=time_peer):
                    by_rows(
                        time_peer == tm - 1,
                        lambda n: wait_landed(c, slot, side, "height", peer, n),
                    )
                    heads_of(c, slot, side)

        @pl.loop(c * HEADS_PER_CHUNK, (c + 1) * HEADS_PER_CHUNK)
        def _(head):
            value = jnp.where(query_ok, acc[head] / total[head], 0.0)
            cols = pl.ds(pl.multiple_of(head * HD, HD), HD)
            att[:, cols] = value.astype(jnp.bfloat16)

    for c in range(chunks):
        for side, peer, there, _ in highs:
            @pl.when(there)
            def _(c=c, side=side, peer=peer):
                wait_landed(c, 0, side, "height", peer, tile)
                heads_of(c, 0, side)
        for slot, peer, there, _ in times:
            @pl.when(there)
            def _(c=c, slot=slot, peer=peer):
                by_rows(
                    peer == tm - 1, lambda n: wait_landed(c, slot, 1, "tm", peer, n)
                )
                for side, high_peer, near, there_side in highs:
                    @pl.when(near)
                    def _(side=side, high_peer=high_peer, there_side=there_side):
                        by_rows(
                            peer == tm - 1,
                            lambda n: high_copy(
                                c, slot, side, high_peer, there_side, n
                            ).start(),
                        )
                heads_of(c, slot, 1)
        if c > 0:
            corners(c - 1)
    corners(chunks - 1)

    w_copy.wait()
    step_rows = tile // ROW_CHUNKS
    live = jnp.where(last_time, pl.cdiv(short, step_rows), ROW_CHUNKS)
    block = w_ref.shape[1] // mp

    def rows_of(r):
        return pl.ds(pl.multiple_of(r * step_rows, step_rows), step_rows)

    def part(d, r):
        if isinstance(d, int):
            columns = pl.ds(d * block, block)
        else:
            columns = pl.ds(pl.multiple_of(d * block, block), block)
        return jnp.dot(att[rows_of(r), :], w_ref[:, columns], preferred_element_type=jnp.float32)

    def right_copy(d, r):
        return pltpu.make_async_remote_copy(
            src_ref=right_out.at[d, rows_of(r)], dst_ref=right_in.at[d, rows_of(r)],
            send_sem=right_send.at[d, r], recv_sem=right_recv.at[d, r],
            device_id={"mp": m + 1}, device_id_type=MESH,
        )

    def left_copy(d, r):
        return pltpu.make_async_remote_copy(
            src_ref=left_out.at[d, rows_of(r)], dst_ref=left_in.at[d, rows_of(r)],
            send_sem=left_send.at[d, r], recv_sem=left_recv.at[d, r],
            device_id={"mp": m - 1}, device_id_type=MESH,
        )

    def stream_step(step, to_right):
        k, r = step // ROW_CHUNKS, step % ROW_CHUNKS
        if to_right:
            d, out, arrived, copy = mp - 1 - k, right_out, right_in, right_copy
            sends, inner = m < d, m > 0
        else:
            d, out, arrived, copy = k, left_out, left_in, left_copy
            sends, inner = m > d, m < mp - 1

        @pl.when(jnp.logical_and(sends, r < live))
        def _():
            final[...] = part(d, r)

            @pl.when(inner)
            def _():
                copy(d, r).wait_recv()
                final[...] += arrived[d, rows_of(r), :].astype(jnp.float32)

            out[d, rows_of(r), :] = final[...].astype(jnp.bfloat16)
            copy(d, r).start()

    steps = (mp - 1) * ROW_CHUNKS
    for near, right_first in ((m < mp // 2, True), (m >= mp // 2, False)):
        @pl.when(near)
        def _(right_first=right_first):
            @pl.loop(0, steps + LEAD)
            def _(step):
                @pl.when(step < steps)
                def _():
                    stream_step(step, right_first)

                @pl.when(step >= LEAD)
                def _():
                    stream_step(step - LEAD, not right_first)

    res_copy.wait()

    @pl.loop(0, ROW_CHUNKS)
    def _(r):
        final[...] = part(m, r)
        for arrived, sem, side, there in (
            (right_in, right_recv, -1, m > 0), (left_in, left_recv, 1, m < mp - 1)
        ):
            @pl.when(jnp.logical_and(there, r < live))
            def _(arrived=arrived, sem=sem, side=side):
                ref = arrived.at[m, rows_of(r)]
                pltpu.make_async_remote_copy(
                    src_ref=ref, dst_ref=ref,
                    send_sem=local_sem.at[0], recv_sem=sem.at[m, r],
                    device_id={"mp": m + side}, device_id_type=MESH,
                ).wait_recv()
                final[...] += arrived[m, rows_of(r), :].astype(jnp.float32)
        value = res_ref[rows_of(r), :].astype(jnp.float32) + gate_ref[...][None, :] * final[...]
        out_ref[rows_of(r), :] = value.astype(jnp.bfloat16)

    for step in range(1, tm):
        text_copy(step).wait_send()
        text_forward(step, parity).wait_send()
    for c in range(chunks):
        for slot, peer, there, there_slot in times:
            @pl.when(there)
            def _(c=c, slot=slot, peer=peer, there_slot=there_slot):
                by_rows(
                    last_time, lambda n: time_copy(c, slot, peer, there_slot, n).wait_send()
                )
        for side, peer, near, there_side in highs:
            @pl.when(near)
            def _(c=c, side=side, peer=peer, there_side=there_side):
                high_copy(c, 0, side, peer, there_side, tile).wait_send()
                for slot, time_peer, there, _ in times:
                    @pl.when(there)
                    def _(slot=slot, time_peer=time_peer):
                        by_rows(
                            time_peer == tm - 1,
                            lambda n: high_copy(
                                c, slot, side, peer, there_side, n
                            ).wait_send(),
                        )
    for k in range(mp - 1):
        @pl.loop(0, ROW_CHUNKS)
        def _(r, k=k):
            @pl.when(jnp.logical_and(m < mp - 1 - k, r < live))
            def _():
                right_copy(mp - 1 - k, r).wait_send()

            @pl.when(jnp.logical_and(m > k, r < live))
            def _():
                left_copy(k, r).wait_send()


def per_device(image_q, image_kv, text_kv, residual, out_weight, out_gate, head_reach, tile_extent):
    tm, height, mp = (lax.axis_size(axis) for axis in ("tm", "height", "mp"))
    tile, width = image_q.shape[2:]
    heads = width // HD
    chunks = heads // HEADS_PER_CHUNK
    slots = min(tm, 3)
    block = residual.shape[3]
    text = text_kv.shape[1] * tm
    half = jnp.bfloat16
    dma = pltpu.SemaphoreType.DMA
    vmem = pl.BlockSpec(memory_space=pltpu.VMEM)
    smem = pl.BlockSpec(memory_space=pltpu.SMEM)
    anywhere = pl.BlockSpec(memory_space=pl.ANY)
    result = pl.pallas_call(
        functools.partial(kernel, (tm, height, mp, slots)),
        out_shape=jax.ShapeDtypeStruct((tile, block), half),
        in_specs=[vmem, anywhere, anywhere, anywhere, anywhere, vmem, smem, smem],
        out_specs=vmem,
        scratch_shapes=[
            pltpu.VMEM((slots, 3, 2, tile, width), half),
            pltpu.VMEM((2, text, width), half),
            pltpu.VMEM(out_weight.shape, half),
            pltpu.VMEM((tile, block), half),
            pltpu.VMEM((tile, width), half),
            pltpu.VMEM((heads, tile, HD), jnp.float32),
            pltpu.VMEM((heads, tile, 1), jnp.float32),
            pltpu.VMEM((heads, tile, 1), jnp.float32),
            pltpu.VMEM((tile // ROW_CHUNKS, block), jnp.float32),
        ]
        + [pltpu.VMEM((mp, tile, block), half)] * 4
        + [
            dma((4,)), dma((tm,)), dma((tm,)), dma((tm,)), dma((tm,)),
            dma((slots, chunks)), dma((slots, 3, chunks)), dma((slots, 3, chunks)),
        ]
        + [dma((mp, ROW_CHUNKS))] * 4,
        compiler_params=pltpu.CompilerParams(
            collective_id=0, has_side_effects=True, vmem_limit_bytes=56 * 2**20
        ),
        cost_estimate=pl.CostEstimate(
            flops=6 * 10**9, bytes_accessed=8 * 10**6, transcendentals=6 * 10**6
        ),
    )(
        image_q.reshape(tile, width),
        image_kv.reshape(2, tile, width),
        text_kv,
        residual.reshape(tile, block),
        out_weight,
        out_gate,
        head_reach.T,
        tile_extent,
    )
    return result.reshape(residual.shape)


def solution(mesh):
    return jax.shard_map(
        per_device,
        mesh=mesh,
        in_specs=(
            P("tm", "height", None, "mp"),
            P("tm", "height", None, None, "mp"),
            P(None, "tm", "mp"),
            P("tm", "height", None, "mp"),
            P("mp", None),
            P("mp"),
            P("mp", None),
            P(),
        ),
        out_specs=P("tm", "height", None, "mp"),
        check_vma=False,
    )
```
